128 devices in a mesh: dp: 16 (over x_lo, y, core), tensor: 8 (over x_hi, z).
Axes of the slice: x: 4 (x_hi: 2, x_lo: 2; x = x_hi * 2 + x_lo), y: 4, z: 4, core: 2. Of those that a mesh axis runs over, the one named last changes fastest.
Arguments:
- hidden: bfloat16 [12288, 12288], P('dp', 'tensor'), may hold values from -6 to 6
- residual_in: bfloat16 [12288, 6144], P('dp', 'tensor'), may hold values from -6 to 6
- w_down: bfloat16 [12288, 6144], P('tensor', 'dp'), may hold values from -0.0546875 to 0.0546875
- w_key: bfloat16 [6144, 2048], P('tensor', 'dp'), may hold values from -0.078125 to 0.078125
- w_value: bfloat16 [6144, 2048], P('tensor', 'dp'), may hold values from -0.078125 to 0.078125
- queries: float32 [512, 2048], P('dp'), may hold values from -6 to 6
- w_query: bfloat16 [2048, 2048], P(None, 'tensor'), may hold values from -0.125 to 0.125
- attn_bias: float32 [16, 32, 768], P('dp'), as said below
- w_out: bfloat16 [2048, 2048], replicated, may hold values from -0.125 to 0.125
- w_in: bfloat16 [2048, 8192], P(None, 'tensor'), may hold values from -0.125 to 0.125
- w_back: bfloat16 [8192, 2048], P('tensor'), may hold values from -0.0625 to 0.0625
Outputs:
- query_out: bfloat16 [512, 2048], P('dp')
The draws below stay inside these ranges and needn't reach their ends.
Inputs may be any that keep to these rules, and one draw needn't show every extreme that they name: `attn_bias`: the same bias for every head of an image.
All inputs are finite; a program needn't handle non-finite values.
Results may differ from the reference program's by a relative error of at most 0.024.
Values may be sent and summed in bfloat16 or wider, within the bound.
No kernel may reach another device: no remote copies, remote signals or barrier semaphores. Data moves between devices by JAX's collectives and lax.ppermute only.
A program may use at most 192 MiB of HBM per device.

```python
import jax
import jax.numpy as jnp
from jax import lax

D = 6144
FF = 12288
HEADS = 16
HEAD_DIM = 128
QD = 2048
QFF = 8192
NQ = 32
TOK = 768
IMAGES = 16
TOKENS = 12288
N_TENSOR = 8


def draw_attn_bias(key, part):
    key = jax.random.fold_in(key, 7)
    base_key = jax.random.fold_in(key, 0)
    shape = (IMAGES, NQ, TOK)
    return jnp.clip(jax.random.normal(base_key, shape, jnp.float32), -4.0, 4.0)


def levels(rng, shape, shards, low, top_value):
    factor_of = 1.0
    for dim, shards_of in shards:
        heights = jax.random.uniform(jax.random.fold_in(jax.random.fold_in(rng, 6), dim), (shards_of,), jnp.float32, low / len(shards), top_value / len(shards))
        factor_of = factor_of * jnp.repeat(jnp.exp(heights), shape[dim] // shards_of).reshape((-1,) + (1,) * (len(shape) - 1 - dim))
    return factor_of


def centred(rng, dims, scale, most, pieces=(), held_as=jnp.bfloat16):
    drawn = jax.random.normal(rng, dims, jnp.float32) * scale
    if len(pieces) > 0:
        drawn = levels(rng, dims, pieces, -0.22, 0.18) * drawn
    return jnp.clip(drawn, min=-most, max=most).astype(held_as)


def setup_inputs(seed: int = 0) -> dict:
    seeds = jax.random.split(jax.random.key(seed), 12)
    hidden = centred(seeds[0], (TOKENS, FF), 1.0, 6.0, ((0, 16), (1, 8)))
    residual_in = centred(seeds[1], (TOKENS, D), 1.0, 6.0, ((0, 16), (1, 8)))
    w_down = centred(seeds[2], (FF, D), FF ** -0.5, 0.0546875, ((0, 8), (1, 16)))
    w_key = centred(seeds[3], (D, QD), D ** -0.5, 0.078125, ((0, 8), (1, 16)))
    w_value = centred(seeds[4], (D, QD), D ** -0.5, 0.078125, ((0, 8), (1, 16)))
    queries = centred(seeds[5], (IMAGES * NQ, QD), 1.0, 6.0, ((0, 16),), jnp.float32)
    w_query = centred(seeds[6], (QD, QD), QD ** -0.5, 0.125, ((1, 8),))
    attn_bias = draw_attn_bias(jax.random.fold_in(seeds[11], 71), 0)
    w_out = centred(seeds[8], (QD, QD), QD ** -0.5, 0.125)
    w_in = centred(seeds[9], (QD, QFF), QD ** -0.5, 0.125, ((1, 8),))
    w_back = centred(seeds[10], (QFF, QD), QFF ** -0.5, 0.0625, ((0, 8),))
    return {"hidden": hidden, "residual_in": residual_in, "w_down": w_down, "w_key": w_key, "w_value": w_value, "queries": queries, "w_query": w_query, "attn_bias": attn_bias, "w_out": w_out, "w_in": w_in, "w_back": w_back}


def layer_norm(x):
    mean = lax.optimization_barrier(jnp.mean(x, axis=-1, keepdims=True))
    centered = x - mean
    var = lax.optimization_barrier(jnp.mean(centered * centered, axis=-1, keepdims=True))
    return centered * lax.rsqrt(var + 1e-06)

def reference(hidden, residual_in, w_down, w_key, w_value, queries, w_query, attn_bias, w_out, w_in, w_back):
    block = FF // N_TENSOR
    scale = 1.0 / HEAD_DIM ** 0.5

    def one_image(index):
        rows = lax.dynamic_slice_in_dim(hidden, (index * TOK).astype(jnp.int32), TOK, 0)
        resid = lax.dynamic_slice_in_dim(residual_in, (index * TOK).astype(jnp.int32), TOK, 0)
        total = resid.astype(jnp.float32)
        for blk in range(N_TENSOR):
            part = jnp.dot(rows[:, blk * block:(blk + 1) * block], w_down[blk * block:(blk + 1) * block], preferred_element_type=jnp.float32)
            part = lax.optimization_barrier(part.astype(jnp.bfloat16))
            total = total + part.astype(jnp.float32)
        features = total.astype(jnp.bfloat16)
        keys = jnp.dot(features, w_key, preferred_element_type=jnp.float32).astype(jnp.bfloat16)
        vals = jnp.dot(features, w_value, preferred_element_type=jnp.float32).astype(jnp.bfloat16)
        query_rows = lax.dynamic_slice_in_dim(queries, (index * NQ).astype(jnp.int32), NQ, 0)
        qnorm = layer_norm(query_rows).astype(jnp.bfloat16)
        qproj = (jnp.dot(qnorm, w_query, preferred_element_type=jnp.float32) * scale).astype(jnp.bfloat16)
        bias = attn_bias[index]
        qh = qproj.astype(jnp.float32).reshape(NQ, HEADS, HEAD_DIM)
        kh = keys.astype(jnp.float32).reshape(TOK, HEADS, HEAD_DIM)
        vh = vals.astype(jnp.float32).reshape(TOK, HEADS, HEAD_DIM)
        scores = jnp.einsum('qhd,khd->hqk', qh, kh) + bias[None]
        probs = jax.nn.softmax(scores, axis=-1).astype(jnp.bfloat16)
        attended = jnp.einsum('hqk,khd->qhd', probs.astype(jnp.float32), vh).astype(jnp.bfloat16).reshape(NQ, QD)
        mid = query_rows + jnp.dot(attended, w_out, preferred_element_type=jnp.float32)
        mnorm = layer_norm(mid).astype(jnp.bfloat16)
        inner = jax.nn.gelu(jnp.dot(mnorm, w_in, preferred_element_type=jnp.float32)).astype(jnp.bfloat16)
        return (mid + jnp.dot(inner, w_back, preferred_element_type=jnp.float32)).astype(jnp.bfloat16)
    result = lax.map(one_image, jnp.arange(IMAGES, dtype=jnp.int32))
    return result.reshape(IMAGES * NQ, QD)
```

```python
import jax
import jax.numpy as jnp
from jax import lax
from jax.sharding import PartitionSpec as P

HEAD_DIM = 128
AXES = ("dp", "tensor")
BF16 = jnp.bfloat16
F32 = jnp.float32


def layer_norm(x):
    mean = jnp.mean(x, axis=-1, keepdims=True)
    centered = x - mean
    var = jnp.mean(centered * centered, axis=-1, keepdims=True)
    return centered * lax.rsqrt(var + 1e-06)


def matmul(a, b):
    return jnp.dot(a, b, preferred_element_type=F32)


def matmul_t(a, b):
    return lax.dot_general(a, b, (((1,), (1,)), ((), ())), preferred_element_type=F32)


def tensor_blocks(x):
    pairs = [[(s, s ^ j) for s in range(8)] for j in range(8)]
    return [x] + [lax.ppermute(x, "tensor", pairs[j]) for j in range(1, 8)]


def tree_sum(blocks):
    while len(blocks) > 1:
        blocks = [a + b for a, b in zip(blocks[::2], blocks[1::2])]
    return blocks[0]


def in_order(blocks):
    me = lax.axis_index("tensor")
    stacked = jnp.stack(blocks)
    return jnp.stack(
        [lax.dynamic_index_in_dim(stacked, me ^ g, 0, keepdims=False) for g in range(8)]
    )


def shards(
    hidden, residual_in, w_down, w_key, w_value, queries, w_query, attn_bias, w_out, w_in, w_back
):
    nq = queries.shape[0]
    ff = hidden.shape[1]
    scale = 1.0 / HEAD_DIM**0.5
    qnorm = layer_norm(queries).astype(BF16)
    qproj = (matmul(qnorm, w_query) * scale).astype(BF16)
    q_heads = in_order(tensor_blocks(qproj))
    q_heads = q_heads.reshape(8, nq, 2, HEAD_DIM).transpose(0, 2, 1, 3).reshape(16 * nq, HEAD_DIM)
    q_all = lax.all_to_all(q_heads, "dp", 0, 0, tiled=True)
    w_kv = jnp.concatenate([w_key, w_value], axis=1)
    down_all = lax.all_gather(w_down, "dp", axis=1, tiled=True)
    kv_all = lax.all_gather(w_kv, "tensor", axis=0, tiled=True)
    w_head = jnp.concatenate([matmul(down_all, kv_all).astype(BF16), w_kv], axis=0)
    q_wide = matmul_t(q_all, w_head[:, :HEAD_DIM]).astype(BF16)
    q_wide = lax.all_to_all(q_wide, "dp", 0, 0, tiled=True)
    part = matmul_t(q_wide[:, :ff], hidden) + matmul_t(q_wide[:, ff:], residual_in)
    part = lax.all_to_all(part.astype(BF16), "tensor", 0, 0, tiled=True)
    scores = jnp.sum(part.reshape(8, 2, nq, -1).astype(F32), axis=0) + attn_bias[0][None]
    probs = jax.nn.softmax(scores, axis=-1).astype(BF16).reshape(2 * nq, -1)
    probs = in_order(tensor_blocks(probs)).reshape(16 * nq, -1)
    wide = jnp.concatenate([matmul(probs, hidden), matmul(probs, residual_in)], axis=1)
    wide = lax.all_to_all(wide.astype(BF16), "dp", 0, 0, tiled=True)
    part = matmul(wide, w_head[:, HEAD_DIM:]).astype(BF16)
    part = lax.all_to_all(part, "dp", 0, 0, tiled=True)
    part = part.reshape(16, nq, HEAD_DIM).transpose(1, 0, 2).reshape(nq, 16 * HEAD_DIM)
    attended = tree_sum([b.astype(F32) for b in tensor_blocks(part)]).astype(BF16)
    mid = queries + matmul(attended, w_out)
    mnorm = layer_norm(mid).astype(BF16)
    inner = jax.nn.gelu(matmul(mnorm, w_in)).astype(BF16)
    back = tensor_blocks(matmul(inner, w_back).astype(BF16))
    return (mid + tree_sum([b.astype(F32) for b in back])).astype(BF16)


def solution(mesh):
    in_specs = (
        P("dp", "tensor"),
        P("dp", "tensor"),
        P("tensor", "dp"),
        P("tensor", "dp"),
        P("tensor", "dp"),
        P("dp", None),
        P(None, "tensor"),
        P("dp", None, None),
        P(),
        P(None, "tensor"),
        P("tensor", None),
    )
    out_specs = P("dp", None)
    return jax.shard_map(shards, mesh=mesh, in_specs=in_specs, out_specs=out_specs, check_vma=False)
```

```python
import jax
import jax.numpy as jnp
from jax import lax
from jax.sharding import PartitionSpec as P

HEAD_DIM = 128
AXES = ("dp", "tensor")
BF16 = jnp.bfloat16
F32 = jnp.float32


def layer_norm(x):
    mean = jnp.mean(x, axis=-1, keepdims=True)
    centered = x - mean
    var = jnp.mean(centered * centered, axis=-1, keepdims=True)
    return centered * lax.rsqrt(var + 1e-06)


def matmul(a, b):
    return jnp.dot(a, b, preferred_element_type=F32)


def matmul_t(a, b):
    return lax.dot_general(a, b, (((1,), (1,)), ((), ())), preferred_element_type=F32)


def tensor_blocks(x):
    pairs = [[(s, s ^ j) for s in range(8)] for j in range(8)]
    return [x] + [lax.ppermute(x, "tensor", pairs[j]) for j in range(1, 8)]


def tree_sum(blocks):
    while len(blocks) > 1:
        blocks = [a + b for a, b in zip(blocks[::2], blocks[1::2])]
    return blocks[0]


def in_order(blocks):
    me = lax.axis_index("tensor")
    stacked = jnp.stack(blocks)
    return jnp.stack(
        [lax.dynamic_index_in_dim(stacked, me ^ g, 0, keepdims=False) for g in range(8)]
    )


def doubling_blocks(x):
    got = x[None]
    for bit in range(3):
        got = jnp.concatenate(
            [got, lax.ppermute(got, "tensor", [(s, s ^ (1 << bit)) for s in range(8)])], axis=0
        )
    return [got[j] for j in range(8)]


def shifts(move):
    pairs = []
    for s in range(128):
        d, t = s // 8, s % 8
        to = move(t // 4, d // 8, d // 2 % 4, t % 4, d % 2)
        if to is not None:
            xh, xl, y, z, c = to
            pairs.append((s, ((xl * 4 + y % 4) * 2 + c) * 8 + xh * 4 + z % 4))
    return pairs


def send(x, pairs):
    return lax.ppermute(x, AXES, pairs)


OTHER_CORE = shifts(lambda xh, xl, y, z, c: (xh, xl, y, z, 1 - c))
X_LO = shifts(lambda xh, xl, y, z, c: (xh, 1 - xl, y, z, c))
Y_UP = shifts(lambda xh, xl, y, z, c: (xh, xl, y + 1, z, c))
Y_DOWN = shifts(lambda xh, xl, y, z, c: (xh, xl, y + 3, z, c))
Z_UP = shifts(lambda xh, xl, y, z, c: (xh, xl, y, z + 1, c))
Z_DOWN = shifts(lambda xh, xl, y, z, c: (xh, xl, y, z + 3, c))
X_FIRST = shifts(lambda xh, xl, y, z, c: ((1, 0), (0, 0), (1, 1), (0, 1))[2 * xh + xl] + (y, z, c))
X_SECOND = shifts(lambda xh, xl, y, z, c: (1 - xh, 1 - xl, y, z, c) if xh != xl else None)


def ring_gather(x, up, down):
    half = x.shape[0] // 2
    below = send(x, up)
    above = send(x, down)
    far = [send(below[:half], up), send(above[half:], down)]
    return [x, above, jnp.concatenate(far, axis=0), below]


def shards(
    hidden, residual_in, w_down, w_key, w_value, queries, w_query, attn_bias, w_out, w_in, w_back
):
    nq = queries.shape[0]
    ff = hidden.shape[1]
    d, t = lax.axis_index("dp"), lax.axis_index("tensor")
    core, y, x_lo = d % 2, d // 2 % 4, d // 8
    z, x_hi = t % 4, t // 4
    scale = 1.0 / HEAD_DIM**0.5
    qnorm = layer_norm(queries).astype(BF16)
    qproj = (matmul(qnorm, w_query) * scale).astype(BF16)
    q_heads = in_order(doubling_blocks(qproj))
    q_heads = q_heads.reshape(8, nq, 2, HEAD_DIM).transpose(0, 2, 1, 3).reshape(16 * nq, HEAD_DIM)
    q_all = lax.all_to_all(q_heads, "dp", 0, 0, tiled=True)
    rows = w_key.shape[0] // 2
    kv = jnp.concatenate([w_key, w_value], axis=1)
    mine = lax.dynamic_slice_in_dim(kv, core * rows, rows, 0)
    got = send(lax.dynamic_slice_in_dim(kv, (1 - core) * rows, rows, 0), OTHER_CORE)
    both = jnp.concatenate(
        [mine[:, :HEAD_DIM], got[:, :HEAD_DIM], mine[:, HEAD_DIM:], got[:, HEAD_DIM:]], axis=1
    )
    first, second = send(both, X_FIRST), send(both, X_SECOND)
    inner_chip = x_hi == x_lo
    own = jnp.where(inner_chip, both, first)
    other = jnp.where(inner_chip, first, second)
    cut = 2 * HEAD_DIM
    key_rows = jnp.stack(
        ring_gather(jnp.concatenate([own[:, :cut], other[:, :cut]], axis=1), Z_UP, Z_DOWN)
    )
    chunks = 2
    size = ff // chunks
    down = [
        ring_gather(w_down[i * size : (i + 1) * size], Y_UP, Y_DOWN) for i in range(chunks)
    ]

    def product(blocks, stacked):
        total = None
        for r in range(4):
            weights = lax.dynamic_index_in_dim(stacked, (y + r - z) % 4, 0, keepdims=False)
            term = matmul(blocks[r], weights)
            total = term if total is None else total + term
        return total

    def scattered(part):
        e = HEAD_DIM
        away = jnp.concatenate([part[:, e : 2 * e], part[:, 3 * e :]], axis=1).astype(BF16)
        here = jnp.concatenate([part[:, :e], part[:, 2 * e : 3 * e]], axis=1)
        here = here + send(away, OTHER_CORE).astype(F32)
        moved = send(here[:, e:].astype(BF16), X_LO)
        return (here[:, :e] + moved.astype(F32)).astype(BF16)

    key_head = jnp.concatenate([scattered(product(b, key_rows)) for b in down] + [w_key], axis=0)
    q_wide = matmul_t(q_all, key_head).astype(BF16)
    q_wide = lax.all_to_all(q_wide, "dp", 0, 0, tiled=True)
    value_rows = jnp.concatenate([own[:, cut:], other[:, cut:]], axis=1)
    value_rows, _ = lax.optimization_barrier((value_rows, key_rows))
    value_rows = jnp.stack(ring_gather(value_rows, Z_UP, Z_DOWN))
    value_rows, _ = lax.optimization_barrier((value_rows, key_head))
    value_part = jnp.concatenate([product(b, value_rows) for b in down], axis=0)
    value_head = jnp.concatenate([scattered(value_part), w_value], axis=0)
    part = matmul_t(q_wide[:, :ff], hidden) + matmul_t(q_wide[:, ff:], residual_in)
    part = lax.all_to_all(part.astype(BF16), "tensor", 0, 0, tiled=True)
    scores = jnp.sum(part.reshape(8, 2, nq, -1).astype(F32), axis=0) + attn_bias[0][None]
    probs = jax.nn.softmax(scores, axis=-1).astype(BF16).reshape(2 * nq, -1)
    probs = in_order(tensor_blocks(probs)).reshape(16 * nq, -1)
    probs, value_head = lax.optimization_barrier((probs, value_head))
    wide = jnp.concatenate([matmul(probs, hidden), matmul(probs, residual_in)], axis=1)
    wide = lax.all_to_all(wide.astype(BF16), "dp", 0, 0, tiled=True)
    part = matmul(wide, value_head).astype(BF16)
    part = lax.all_to_all(part, "dp", 0, 0, tiled=True)
    part = part.reshape(16, nq, HEAD_DIM).transpose(1, 0, 2).reshape(nq, 16 * HEAD_DIM)
    attended = tree_sum([b.astype(F32) for b in tensor_blocks(part)]).astype(BF16)
    mid = queries + matmul(attended, w_out)
    mnorm = layer_norm(mid).astype(BF16)
    inner = jax.nn.gelu(matmul(mnorm, w_in)).astype(BF16)
    back = tensor_blocks(matmul(inner, w_back).astype(BF16))
    return (mid + tree_sum([b.astype(F32) for b in back])).astype(BF16)


def solution(mesh):
    in_specs = (
        P("dp", "tensor"),
        P("dp", "tensor"),
        P("tensor", "dp"),
        P("tensor", "dp"),
        P("tensor", "dp"),
        P("dp", None),
        P(None, "tensor"),
        P("dp", None, None),
        P(),
        P(None, "tensor"),
        P("tensor", None),
    )
    out_specs = P("dp", None)
    return jax.shard_map(shards, mesh=mesh, in_specs=in_specs, out_specs=out_specs, check_vma=False)
```

```python
import jax
import jax.numpy as jnp
from jax import lax
from jax.sharding import PartitionSpec as P

HEAD_DIM = 128
AXES = ("dp", "tensor")
BF16 = jnp.bfloat16
F32 = jnp.float32


def layer_norm(x):
    mean = jnp.mean(x, axis=-1, keepdims=True)
    centered = x - mean
    var = jnp.mean(centered * centered, axis=-1, keepdims=True)
    return centered * lax.rsqrt(var + 1e-06)


def matmul(a, b):
    return jnp.dot(a, b, preferred_element_type=F32)


def matmul_t(a, b):
    return lax.dot_general(a, b, (((1,), (1,)), ((), ())), preferred_element_type=F32)


def doubling_blocks(x, arrived):
    got = x[None]
    for bit in range(3):
        if bit == 1:
            got, _ = lax.optimization_barrier((got, arrived))
        got = jnp.concatenate(
            [got, lax.ppermute(got, "tensor", [(s, s ^ (1 << bit)) for s in range(8)])], axis=0
        )
    return [got[j] for j in range(8)]


def shifts(move):
    pairs = []
    for s in range(128):
        d, t = s // 8, s % 8
        to = move(t // 4, d // 8, d // 2 % 4, t % 4, d % 2)
        if to is not None:
            xh, xl, y, z, c = to
            pairs.append((s, ((xl * 4 + y % 4) * 2 + c) * 8 + xh * 4 + z % 4))
    return pairs


def send(x, pairs):
    return lax.ppermute(x, AXES, pairs)


OTHER_CORE = shifts(lambda xh, xl, y, z, c: (xh, xl, y, z, 1 - c))
X_LO = shifts(lambda xh, xl, y, z, c: (xh, 1 - xl, y, z, c))
Y_UP = shifts(lambda xh, xl, y, z, c: (xh, xl, y + 1, z, c))
Y_DOWN = shifts(lambda xh, xl, y, z, c: (xh, xl, y + 3, z, c))
Z_UP = shifts(lambda xh, xl, y, z, c: (xh, xl, y, z + 1, c))
Z_DOWN = shifts(lambda xh, xl, y, z, c: (xh, xl, y, z + 3, c))
X_FIRST = shifts(lambda xh, xl, y, z, c: ((1, 0), (0, 0), (1, 1), (0, 1))[2 * xh + xl] + (y, z, c))
X_SECOND = shifts(lambda xh, xl, y, z, c: (1 - xh, 1 - xl, y, z, c) if xh != xl else None)


def ring_gather(x, up, down):
    half = x.shape[0] // 2
    below = send(x, up)
    above = send(x, down)
    far = [send(below[:half], up), send(above[half:], down)]
    return [x, above, jnp.concatenate(far, axis=0), below]


def in_order(blocks):
    me = lax.axis_index("tensor")
    stacked = jnp.stack(blocks)
    return jnp.stack(
        [lax.dynamic_index_in_dim(stacked, me ^ g, 0, keepdims=False) for g in range(8)]
    )


def tensor_sum(x):
    def from_xor(v, j):
        return lax.ppermute(v, "tensor", [(s, s ^ j) for s in range(8)]).astype(F32)

    x = (x.astype(F32) + from_xor(x, 4)).astype(BF16)
    return (x.astype(F32) + from_xor(x, 1)) + (from_xor(x, 2) + from_xor(x, 3))


def chip_gather(x):
    half = x.shape[0] // 2
    below, above, beside = send(x, Y_UP), send(x, Y_DOWN), send(x, X_LO)
    far = jnp.concatenate([send(below[:half], Y_UP), send(above[half:], Y_DOWN)], axis=0)
    beside_below, beside_above = send(beside, Y_UP), send(beside, Y_DOWN)
    beside_far = send(far, X_LO)
    return [x, above, far, below], [beside, beside_above, beside_far, beside_below]


def shards(
    hidden, residual_in, w_down, w_key, w_value, queries, w_query, attn_bias, w_out, w_in, w_back
):
    nq = queries.shape[0]
    ff = hidden.shape[1]
    e = HEAD_DIM
    d, t = lax.axis_index("dp"), lax.axis_index("tensor")
    core, y, x_lo = d % 2, d // 2 % 4, d // 8
    z, x_hi = t % 4, t // 4
    scale = 1.0 / HEAD_DIM**0.5
    down = ring_gather(w_down, Y_UP, Y_DOWN)
    rows = w_key.shape[0] // 2
    kv = jnp.concatenate([w_key, w_value], axis=1)
    mine = lax.dynamic_slice_in_dim(kv, core * rows, rows, 0)
    got = send(lax.dynamic_slice_in_dim(kv, (1 - core) * rows, rows, 0), OTHER_CORE)
    both = jnp.concatenate([mine[:, :e], got[:, :e], mine[:, e:], got[:, e:]], axis=1)
    first, second = send(both, X_FIRST), send(both, X_SECOND)
    inner_chip = x_hi == x_lo
    own = jnp.where(inner_chip, both, first)
    other = jnp.where(inner_chip, first, second)
    pieces = [a[:, i * e : (i + 1) * e] for i in range(4) for a in (own, other)]
    kv_rows = jnp.concatenate(pieces, axis=1)
    qnorm = layer_norm(queries).astype(BF16)
    qproj = (matmul(qnorm, w_query) * scale).astype(BF16)
    q_heads = in_order(doubling_blocks(qproj, (first, second)))
    q_heads = q_heads.reshape(8, nq, 2, e).transpose(0, 2, 1, 3).reshape(16 * nq, e)
    q_all = lax.all_to_all(q_heads, "dp", 0, 0, tiled=True)
    half = rows // 2
    below, above = send(kv_rows, Z_UP), send(kv_rows, Z_DOWN)
    (below, above), q_all = lax.optimization_barrier(((below, above), q_all))
    far = jnp.concatenate([send(below[:half], Z_UP), send(above[half:], Z_DOWN)], axis=0)
    kv_rows = jnp.stack([kv_rows, above, far, below])

    def product(blocks, stacked):
        total = None
        for r in range(4):
            weights = lax.dynamic_index_in_dim(stacked, (y + r - z) % 4, 0, keepdims=False)
            term = matmul(blocks[r], weights)
            total = term if total is None else total + term
        return total

    def core_sum(part):
        return part[:, : 2 * e] + send(part[:, 2 * e :].astype(BF16), OTHER_CORE).astype(F32)

    def x_sum(here):
        return (here[:, :e] + send(here[:, e:].astype(BF16), X_LO).astype(F32)).astype(BF16)

    cut = 4 * e
    key_rows, value_rows = kv_rows[:, :, :cut], kv_rows[:, :, cut:]
    key_sum = core_sum(product(down, key_rows))
    value_rows, key_sum = lax.optimization_barrier((value_rows, key_sum))
    key_head = jnp.concatenate([x_sum(key_sum), w_key], axis=0)
    value_head = jnp.concatenate([x_sum(core_sum(product(down, value_rows))), w_value], axis=0)
    wide = lax.all_to_all(matmul_t(q_all, key_head).astype(BF16), "dp", 0, 0, tiled=True)
    value_head, wide = lax.optimization_barrier((value_head, wide))
    near, beside = chip_gather(value_head)
    values = [jnp.stack(near), jnp.stack(beside)]
    values = values + [send(v, OTHER_CORE) for v in values]
    part = matmul_t(wide[:, :ff], hidden) + matmul_t(wide[:, ff:], residual_in)
    part = lax.all_to_all(part.astype(BF16), "tensor", 0, 0, tiled=True)
    scores = jnp.sum(part.reshape(8, 2, nq, -1).astype(F32), axis=0) + attn_bias[0][None]
    probs = jax.nn.softmax(scores, axis=-1).astype(BF16).reshape(1, 2 * nq, -1)
    probs = jnp.broadcast_to(probs, (8,) + probs.shape[1:]).reshape(16 * nq, -1)
    probs = lax.all_to_all(probs, "tensor", 0, 0, tiled=True)
    def head_of(k):
        return ((x_lo ^ (k // 4 % 2)) * 4 + (y + k) % 4) * 2 + (core ^ (k // 8))

    row = lax.broadcasted_iota(jnp.int32, (16 * nq, 16 * nq), 0)
    column = lax.broadcasted_iota(jnp.int32, (16 * nq, 16 * nq), 1)
    moves = (head_of(row // nq) * nq + row % nq == column).astype(BF16)
    probs = matmul(moves, probs).astype(BF16)
    wide = jnp.concatenate([matmul(probs, hidden), matmul(probs, residual_in)], axis=1)
    wide = wide.astype(BF16).reshape(4, 4, nq, -1)
    part = [
        lax.dot_general(wide[i], values[i], (((2,), (1,)), ((0,), (0,))), preferred_element_type=F32)
        for i in range(4)
    ]
    part = jnp.concatenate(part, axis=0).astype(BF16)
    places = [
        (core ^ (h % 2)) * 8 + (x_lo ^ (h // 8)) * 4 + (h // 2 - y) % 4 for h in range(16)
    ]
    part = jnp.concatenate(
        [lax.dynamic_index_in_dim(part, k, 0, keepdims=False) for k in places], axis=1
    )
    attended = tensor_sum(part).astype(BF16)
    mid = queries + matmul(attended, w_out)
    mnorm = layer_norm(mid).astype(BF16)
    inner = jax.nn.gelu(matmul(mnorm, w_in)).astype(BF16)
    back = tensor_sum(matmul(inner, w_back).astype(BF16))
    return (mid + back).astype(BF16)


def solution(mesh):
    in_specs = (
        P("dp", "tensor"),
        P("dp", "tensor"),
        P("tensor", "dp"),
        P("tensor", "dp"),
        P("tensor", "dp"),
        P("dp", None),
        P(None, "tensor"),
        P("dp", None, None),
        P(),
        P(None, "tensor"),
        P("tensor", None),
    )
    out_specs = P("dp", None)
    return jax.shard_map(shards, mesh=mesh, in_specs=in_specs, out_specs=out_specs, check_vma=False)
```

```python
import jax
import jax.numpy as jnp
from jax import lax
from jax.experimental import pallas as pl
from jax.experimental.pallas import tpu as pltpu
from jax.sharding import PartitionSpec as P

HEAD_DIM = 128
AXES = ("dp", "tensor")
BF16 = jnp.bfloat16
F32 = jnp.float32


def layer_norm(x):
    mean = jnp.mean(x, axis=-1, keepdims=True)
    centered = x - mean
    var = jnp.mean(centered * centered, axis=-1, keepdims=True)
    return centered * lax.rsqrt(var + 1e-06)


def matmul(a, b):
    return jnp.dot(a, b, preferred_element_type=F32)


def matmul_t(a, b):
    return lax.dot_general(a, b, (((1,), (1,)), ((), ())), preferred_element_type=F32)


def doubling_blocks(x, arrived):
    got = x[None]
    for bit in range(3):
        if bit == 1:
            got, _ = lax.optimization_barrier((got, arrived))
        got = jnp.concatenate(
            [got, lax.ppermute(got, "tensor", [(s, s ^ (1 << bit)) for s in range(8)])], axis=0
        )
    return [got[j] for j in range(8)]


def shifts(move):
    pairs = []
    for s in range(128):
        d, t = s // 8, s % 8
        to = move(t // 4, d // 8, d // 2 % 4, t % 4, d % 2)
        if to is not None:
            xh, xl, y, z, c = to
            pairs.append((s, ((xl * 4 + y % 4) * 2 + c) * 8 + xh * 4 + z % 4))
    return pairs


def send(x, pairs):
    return lax.ppermute(x, AXES, pairs)


OTHER_CORE = shifts(lambda xh, xl, y, z, c: (xh, xl, y, z, 1 - c))
X_LO = shifts(lambda xh, xl, y, z, c: (xh, 1 - xl, y, z, c))
Y_UP = shifts(lambda xh, xl, y, z, c: (xh, xl, y + 1, z, c))
Y_DOWN = shifts(lambda xh, xl, y, z, c: (xh, xl, y + 3, z, c))
Z_UP = shifts(lambda xh, xl, y, z, c: (xh, xl, y, z + 1, c))
Z_DOWN = shifts(lambda xh, xl, y, z, c: (xh, xl, y, z + 3, c))
X_FIRST = shifts(lambda xh, xl, y, z, c: ((1, 0), (0, 0), (1, 1), (0, 1))[2 * xh + xl] + (y, z, c))
X_SECOND = shifts(lambda xh, xl, y, z, c: (1 - xh, 1 - xl, y, z, c) if xh != xl else None)


def ring_gather(x, up, down):
    half = x.shape[0] // 2
    below = send(x, up)
    above = send(x, down)
    far = [send(below[:half], up), send(above[half:], down)]
    return [x, above, jnp.concatenate(far, axis=0), below]


def in_order(blocks):
    me = lax.axis_index("tensor")
    stacked = jnp.stack(blocks)
    return jnp.stack(
        [lax.dynamic_index_in_dim(stacked, me ^ g, 0, keepdims=False) for g in range(8)]
    )


def tensor_sum(x):
    def from_xor(v, j):
        return lax.ppermute(v, "tensor", [(s, s ^ j) for s in range(8)]).astype(F32)

    x = (x.astype(F32) + from_xor(x, 4)).astype(BF16)
    return (x.astype(F32) + from_xor(x, 1)) + (from_xor(x, 2) + from_xor(x, 3))


def chip_gather(x):
    half = x.shape[0] // 2
    below, above, beside = send(x, Y_UP), send(x, Y_DOWN), send(x, X_LO)
    far = jnp.concatenate([send(below[:half], Y_UP), send(above[half:], Y_DOWN)], axis=0)
    beside_below, beside_above = send(beside, Y_UP), send(beside, Y_DOWN)
    beside_far = send(far, X_LO)
    return [x, above, far, below], [beside, beside_above, beside_far, beside_below]


def back_kernel(inner, weights, out, held, arrived):
    pieces = held.shape[0]
    rows = held.shape[1]
    copies = [
        pltpu.make_async_copy(weights.at[pl.ds(k * rows, rows)], held.at[k], arrived.at[k])
        for k in range(pieces)
    ]
    for copy in copies:
        copy.start()
    total = None
    for k in range(pieces):
        copies[k].wait()
        part = matmul(inner[:, k * rows : (k + 1) * rows], held[k])
        total = part if total is None else total + part
    out[...] = total.astype(out.dtype)


def back_project(inner, weights):
    pieces = 4
    depth, width = weights.shape
    vmem = pl.BlockSpec(memory_space=pltpu.VMEM)
    return pl.pallas_call(
        back_kernel,
        out_shape=jax.ShapeDtypeStruct((inner.shape[0], width), BF16),
        in_specs=[vmem, pl.BlockSpec(memory_space=pl.ANY)],
        out_specs=vmem,
        scratch_shapes=[
            pltpu.VMEM((pieces, depth // pieces, width), BF16),
            pltpu.SemaphoreType.DMA((pieces,)),
        ],
        compiler_params=pltpu.CompilerParams(vmem_limit_bytes=24 * 2**20),
        cost_estimate=pl.CostEstimate(
            flops=2 * inner.shape[0] * depth * width,
            bytes_accessed=2 * depth * width,
            transcendentals=0,
        ),
    )(inner, weights)


def shards(
    hidden, residual_in, w_down, w_key, w_value, queries, w_query, attn_bias, w_out, w_in, w_back
):
    nq = queries.shape[0]
    ff = hidden.shape[1]
    e = HEAD_DIM
    d, t = lax.axis_index("dp"), lax.axis_index("tensor")
    core, y, x_lo = d % 2, d // 2 % 4, d // 8
    z, x_hi = t % 4, t // 4
    scale = 1.0 / HEAD_DIM**0.5
    down = ring_gather(w_down, Y_UP, Y_DOWN)
    rows = w_key.shape[0] // 2
    kv = jnp.concatenate([w_key, w_value], axis=1)
    mine = lax.dynamic_slice_in_dim(kv, core * rows, rows, 0)
    got = send(lax.dynamic_slice_in_dim(kv, (1 - core) * rows, rows, 0), OTHER_CORE)
    both = jnp.concatenate([mine[:, :e], got[:, :e], mine[:, e:], got[:, e:]], axis=1)
    first, second = send(both, X_FIRST), send(both, X_SECOND)
    inner_chip = x_hi == x_lo
    own = jnp.where(inner_chip, both, first)
    other = jnp.where(inner_chip, first, second)
    pieces = [a[:, i * e : (i + 1) * e] for i in range(4) for a in (own, other)]
    kv_rows = jnp.concatenate(pieces, axis=1)
    qnorm = layer_norm(queries).astype(BF16)
    qproj = (matmul(qnorm, w_query) * scale).astype(BF16)
    q_heads = in_order(doubling_blocks(qproj, (first, second)))
    q_heads = q_heads.reshape(8, nq, 2, e).transpose(0, 2, 1, 3).reshape(16 * nq, e)
    q_all = lax.all_to_all(q_heads, "dp", 0, 0, tiled=True)
    half = rows // 2
    below, above = send(kv_rows, Z_UP), send(kv_rows, Z_DOWN)
    (below, above), q_all = lax.optimization_barrier(((below, above), q_all))
    far = jnp.concatenate([send(below[:half], Z_UP), send(above[half:], Z_DOWN)], axis=0)
    kv_rows = jnp.stack([kv_rows, above, far, below])

    def product(blocks, stacked):
        total = None
        for r in range(4):
            weights = lax.dynamic_index_in_dim(stacked, (y + r - z) % 4, 0, keepdims=False)
            term = matmul(blocks[r], weights)
            total = term if total is None else total + term
        return total

    def core_sum(part):
        return part[:, : 2 * e] + send(part[:, 2 * e :].astype(BF16), OTHER_CORE).astype(F32)

    def x_sum(here):
        return (here[:, :e] + send(here[:, e:].astype(BF16), X_LO).astype(F32)).astype(BF16)

    cut = 4 * e
    key_rows, value_rows = kv_rows[:, :, :cut], kv_rows[:, :, cut:]
    key_sum = core_sum(product(down, key_rows))
    value_rows, key_sum = lax.optimization_barrier((value_rows, key_sum))
    key_head = jnp.concatenate([x_sum(key_sum), w_key], axis=0)
    value_head = jnp.concatenate([x_sum(core_sum(product(down, value_rows))), w_value], axis=0)
    wide = lax.all_to_all(matmul_t(q_all, key_head).astype(BF16), "dp", 0, 0, tiled=True)
    value_head, wide = lax.optimization_barrier((value_head, wide))
    near, beside = chip_gather(value_head)
    values = [jnp.stack(near), jnp.stack(beside)]
    values = values + [send(v, OTHER_CORE) for v in values]
    part = matmul_t(wide[:, :ff], hidden) + matmul_t(wide[:, ff:], residual_in)
    part = lax.all_to_all(part.astype(BF16), "tensor", 0, 0, tiled=True)
    scores = jnp.sum(part.reshape(8, 2, nq, -1).astype(F32), axis=0) + attn_bias[0][None]
    probs = jax.nn.softmax(scores, axis=-1).astype(BF16).reshape(1, 2 * nq, -1)
    probs = jnp.broadcast_to(probs, (8,) + probs.shape[1:]).reshape(16 * nq, -1)
    probs = lax.all_to_all(probs, "tensor", 0, 0, tiled=True)
    def head_of(k):
        return ((x_lo ^ (k // 4 % 2)) * 4 + (y + k) % 4) * 2 + (core ^ (k // 8))

    row = lax.broadcasted_iota(jnp.int32, (16 * nq, 16 * nq), 0)
    column = lax.broadcasted_iota(jnp.int32, (16 * nq, 16 * nq), 1)
    moves = (head_of(row // nq) * nq + row % nq == column).astype(BF16)
    probs = matmul(moves, probs).astype(BF16)
    wide = jnp.concatenate([matmul(probs, hidden), matmul(probs, residual_in)], axis=1)
    wide = wide.astype(BF16).reshape(4, 4, nq, -1)
    part = [
        lax.dot_general(wide[i], values[i], (((2,), (1,)), ((0,), (0,))), preferred_element_type=F32)
        for i in range(4)
    ]
    part = jnp.concatenate(part, axis=0).astype(BF16)
    places = [
        (core ^ (h % 2)) * 8 + (x_lo ^ (h // 8)) * 4 + (h // 2 - y) % 4 for h in range(16)
    ]
    part = jnp.concatenate(
        [lax.dynamic_index_in_dim(part, k, 0, keepdims=False) for k in places], axis=1
    )
    attended = tensor_sum(part).astype(BF16)
    mid = queries + matmul(attended, w_out)
    mnorm = layer_norm(mid).astype(BF16)
    inner = jax.nn.gelu(matmul(mnorm, w_in)).astype(BF16)
    back = tensor_sum(back_project(inner, w_back))
    return (mid + back).astype(BF16)


def solution(mesh):
    in_specs = (
        P("dp", "tensor"),
        P("dp", "tensor"),
        P("tensor", "dp"),
        P("tensor", "dp"),
        P("tensor", "dp"),
        P("dp", None),
        P(None, "tensor"),
        P("dp", None, None),
        P(),
        P(None, "tensor"),
        P("tensor", None),
    )
    out_specs = P("dp", None)
    return jax.shard_map(shards, mesh=mesh, in_specs=in_specs, out_specs=out_specs, check_vma=False)
```
